32 devices in a mesh: groups: 2 (over y), tensor: 4 (over z), fsdp: 2 (over x), dp: 2 (over core).
Axes of the slice: x: 2, y: 2, z: 4, core: 2. Of those that a mesh axis runs over, the one named last changes fastest.
Arguments:
- tokens: bfloat16 [8, 256, 8192], P(('groups', 'fsdp', 'dp')), parts along dimension 0, may hold values from -6 to 6
- teacher: bfloat16 [8, 256, 8192], P(('groups', 'fsdp', 'dp')), parts along dimension 0, may hold values from -3 to 3
- in_blocks: bfloat16 [8192, 4608], P('fsdp', 'tensor'), may hold values from -0.09375 to 0.09375
- in_columns: int32 [64, 36], P('fsdp', 'tensor'), may hold values from 0 to 17, as said below
- step_weight: bfloat16 [8192, 128], P('fsdp', 'tensor'), may hold values from -0.0625 to 0.0625
- out_blocks: bfloat16 [8192, 4096], P('fsdp', 'tensor'), may hold values from -0.09375 to 0.09375
- out_columns: int32 [64, 32], P('fsdp', 'tensor'), may hold values from 0 to 15, as said below
- conv_weight: float32 [4, 9216], P(None, 'tensor'), may hold values from -3 to 3
- step_bias: float32 [128], P('tensor'), may hold values from -2 to 0.5
- decay_rate: float32 [128], P('tensor'), may hold values from 0.005 to 0.3
- skip_gain: float32 [128], P('tensor'), may hold values from 0.5 to 1.5
- norm_gain: float32 [8192], P('tensor'), may hold values from 0.5 to 1.5
Outputs:
- sq_error: float32 [8, 256], P(('groups', 'fsdp', 'dp')), parts along dimension 0
- in_grad: float32 [16384, 4608], P(('groups', 'fsdp', 'dp'), 'tensor'), parts along dimension 0
- out_grad: float32 [16384, 4096], P(('groups', 'fsdp', 'dp'), 'tensor'), parts along dimension 0
The draws below stay inside these ranges and needn't reach their ends.
There are 2 independent parts, one for each index of `groups`. The reference program is written for one: setup_inputs(seed, part) draws one part's arguments, and reference() takes and returns one part's arrays. A program takes and returns all parts, laid end to end along the dimension named above; an argument that names none is the same for every part. Nothing has to cross between parts.
Inputs may be any that keep to these rules, and one draw needn't show every extreme that they name: `in_columns`: in every row the 9 entries g * 9 to g * 9 + 8 are distinct, for every group g. `out_columns`: in every row the 8 entries g * 8 to g * 8 + 7 are distinct, for every group g.
All inputs are finite; a program needn't handle non-finite values.
Results may differ from the reference program's by a relative error of at most 0.014.
Values may be sent and summed in bfloat16 or wider, within the bound.
A program may use at most 320 MiB of HBM per device.

```python
import math
import jax
import jax.numpy as jnp
from jax import lax

D = 8192
E = 8192
P_SIZE = 64
BLOCK = 128
KCONV = 4
SEQ = 256
H = 128
CHAN = 9216
KEEP_IN = 9
KEEP_OUT = 8
BATCH = 4
N_TENSOR = 4


def choose_blocks(key, block_rows, group_sets, pool_size, keep_count):
    scores = jax.random.randint(key, (block_rows, group_sets, pool_size), 0, 1 << 20, dtype=jnp.int32)
    scores = scores * pool_size + jnp.arange(pool_size, dtype=jnp.int32)[None, None, :]
    ordered = jnp.argsort(scores, axis=-1, stable=True)
    return ordered[:, :, :keep_count].reshape(block_rows, group_sets * keep_count).astype(jnp.int32)


def draw_in_columns(key, part):
    key = jax.random.fold_in(key, 11)
    return choose_blocks(key, D // BLOCK, N_TENSOR, 2 * KEEP_IN, KEEP_IN)


def draw_out_columns(key, part):
    key = jax.random.fold_in(key, 23)
    return choose_blocks(key, D // BLOCK, N_TENSOR, 2 * KEEP_OUT, KEEP_OUT)


def shard_levels(stream_key, extent, split, least, high):
    def one(position, blocks):
        heights = jax.random.uniform(jax.random.fold_in(jax.random.fold_in(stream_key, 6), position), (blocks,), jnp.float32, least / len(split), high / len(split))
        return jnp.repeat(jnp.exp(heights), extent[position] // blocks).reshape((-1,) + (1,) * (len(extent) - position - 1))

    loudness = one(*split[0])
    for cut in split[1:]:
        loudness = loudness * one(*cut)
    return loudness


def centred(stream_key, dims, scale, limit, split=(), kind=jnp.bfloat16):
    values = jax.random.normal(stream_key, dims, jnp.float32) * scale
    if len(split) > 0:
        values = shard_levels(stream_key, dims, split, -0.22, 0.18) * values
    return jnp.clip(values, min=-limit, max=limit).astype(kind)


def setup_inputs(seed: int = 0, part: int = 0) -> dict:
    keys = jax.random.split(jax.random.key(seed), 13)
    part_splits = jax.random.split(jax.random.fold_in(keys[12], part), 13)
    return {
        "tokens": centred(part_splits[0], (BATCH, SEQ, D), 1.0, 6.0, ((0, 4),)),
        "teacher": centred(part_splits[1], (BATCH, SEQ, D), 0.5, 3.0, ((0, 4),)),
        "in_blocks": centred(keys[2], (D, N_TENSOR * KEEP_IN * BLOCK), (D // 2) ** -0.5, 0.09375, ((0, 2), (1, 4))),
        "in_columns": draw_in_columns(jax.random.fold_in(keys[12], 71), part),
        "step_weight": centred(keys[4], (D, H), D ** -0.5, 0.0625, ((0, 2), (1, 4))),
        "out_blocks": centred(keys[5], (D, N_TENSOR * KEEP_OUT * BLOCK), (E // 2) ** -0.5, 0.09375, ((0, 2), (1, 4))),
        "out_columns": draw_out_columns(jax.random.fold_in(keys[12], 71), part),
        "conv_weight": centred(keys[7], (KCONV, CHAN), 0.5, 3.0, ((1, 4),), jnp.float32),
        "step_bias": jnp.clip(-2.0 + 2.5 * jax.random.uniform(keys[8], (H,), jnp.float32) ** shard_levels(keys[8], (H,), ((0, 4),), -0.2, 0.2), -2.0, 0.5),
        "decay_rate": jnp.clip(jnp.exp(math.log(0.3) - 4.0943446 * jax.random.uniform(keys[9], (H,), jnp.float32) ** shard_levels(keys[9], (H,), ((0, 4),), -0.2, 0.2)), 0.005, 0.3),
        "skip_gain": jnp.clip(0.5 + 1.0 * jax.random.uniform(keys[10], (H,), jnp.float32) ** shard_levels(keys[10], (H,), ((0, 4),), -0.2, 0.2), 0.5, 1.5),
        "norm_gain": jnp.clip(1.0 + 0.1 * jax.random.normal(keys[11], (E,), jnp.float32), 0.5, 1.5),
    }


def spread_blocks(blocks, chosen, group_width):
    block_rows = chosen.shape[0]
    keep_count = chosen.shape[1]
    picked = (chosen[:, :, None] == jnp.arange(group_width, dtype=jnp.int32)[None, None, :]).astype(jnp.float32)
    tile_grid = blocks.astype(jnp.float32).reshape(block_rows, BLOCK, keep_count, BLOCK)
    dense_grid = jnp.einsum('rkc,rikj->ricj', picked, tile_grid)
    return dense_grid.astype(jnp.bfloat16).reshape(block_rows * BLOCK, group_width * BLOCK)

def keep_blocks(dense_grad, chosen):
    block_rows = chosen.shape[0]
    keep_count = chosen.shape[1]
    group_width = dense_grad.shape[1] // BLOCK
    tile_grid = dense_grad.reshape(block_rows, BLOCK, group_width, BLOCK)
    selected = jnp.take_along_axis(tile_grid, chosen[:, None, :, None], axis=2)
    return selected.reshape(block_rows * BLOCK, keep_count * BLOCK)

def state_mixer(projected, step_raw, conv_taps, step_bias, decay_rate, skip_gain, norm_gain):
    seq_steps = projected.shape[0]
    chan_count = projected.shape[1]
    inner_width = norm_gain.shape[0]
    head_count = step_bias.shape[0]
    head_width = inner_width // head_count
    state_size = (chan_count - inner_width) // 2
    taps = conv_taps.shape[0]
    padded = jnp.concatenate([jnp.zeros((taps - 1, chan_count), jnp.float32), projected], 0)
    conv_sum = jnp.zeros((seq_steps, chan_count), jnp.float32)
    for offset in range(taps):
        conv_sum = conv_sum + conv_taps[offset][None, :] * padded[offset:offset + seq_steps]
    activated = jax.nn.silu(conv_sum)
    head_inputs = activated[:, :inner_width].reshape(seq_steps, head_count, head_width)
    state_in = activated[:, inner_width:inner_width + state_size]
    state_out = activated[:, inner_width + state_size:]
    step_size = jax.nn.softplus(step_raw + step_bias[None, :])
    log_decay = jnp.cumsum(-decay_rate[None, :] * step_size, axis=0)
    scores = jnp.dot(state_out, state_in.T, precision=lax.Precision.HIGHEST)
    later = (jnp.arange(seq_steps)[:, None] >= jnp.arange(seq_steps)[None, :])[:, :, None]
    log_gap = log_decay[:, None, :] - log_decay[None, :, :]
    decay = jnp.where(later, jnp.exp(jnp.where(later, log_gap, 0.0)), 0.0)
    weights = scores[:, :, None] * decay * step_size[None, :, :]
    mixed = jnp.einsum('tsh,shp->thp', weights, head_inputs, precision=lax.Precision.HIGHEST)
    mixed = mixed + skip_gain[None, :, None] * head_inputs
    flat = mixed.reshape(seq_steps, inner_width)
    scale = lax.rsqrt(lax.optimization_barrier(jnp.mean(flat * flat, axis=1, keepdims=True)) + 1e-05)
    return flat * scale * norm_gain[None, :]

def reference(tokens, teacher, in_blocks, in_columns, step_weight, out_blocks, out_columns, conv_weight, step_bias, decay_rate, skip_gain, norm_gain):
    chan_count = CHAN // N_TENSOR
    inner_width = E // N_TENSOR
    head_count = inner_width // P_SIZE
    flat_tokens = tokens.reshape(BATCH * SEQ, D)

    def weights_of(group_index):
        in_part = lax.dynamic_slice_in_dim(in_blocks, group_index * (KEEP_IN * BLOCK), KEEP_IN * BLOCK, 1)
        in_pick = lax.dynamic_slice_in_dim(in_columns, group_index * KEEP_IN, KEEP_IN, 1)
        out_part = lax.dynamic_slice_in_dim(out_blocks, group_index * (KEEP_OUT * BLOCK), KEEP_OUT * BLOCK, 1)
        out_pick = lax.dynamic_slice_in_dim(out_columns, group_index * KEEP_OUT, KEEP_OUT, 1)
        w_in = spread_blocks(in_part, in_pick, 2 * KEEP_IN)
        w_out = spread_blocks(out_part, out_pick, 2 * KEEP_OUT)
        w_step = lax.dynamic_slice_in_dim(step_weight, group_index * head_count, head_count, 1)
        taps = lax.dynamic_slice_in_dim(conv_weight, group_index * chan_count, chan_count, 1)
        bias = lax.dynamic_slice_in_dim(step_bias, group_index * head_count, head_count, 0)
        rates = lax.dynamic_slice_in_dim(decay_rate, group_index * head_count, head_count, 0)
        skips = lax.dynamic_slice_in_dim(skip_gain, group_index * head_count, head_count, 0)
        gains = lax.dynamic_slice_in_dim(norm_gain, group_index * inner_width, inner_width, 0)
        return (w_in, w_out, w_step, (taps, bias, rates, skips, gains), in_pick, out_pick)

    def add_group(total, group_index):
        w_in, w_out, w_step, params, in_pick, out_pick = weights_of(group_index)
        projected = jnp.dot(flat_tokens, w_in, preferred_element_type=jnp.float32).astype(jnp.bfloat16)
        step_raw = jnp.dot(flat_tokens, w_step, preferred_element_type=jnp.float32)
        projected = projected.reshape(BATCH, SEQ, chan_count)
        step_raw = step_raw.reshape(BATCH, SEQ, head_count)
        normed = jax.vmap(lambda values, raws: state_mixer(values.astype(jnp.float32), raws, *params))(projected, step_raw)
        normed = normed.astype(jnp.bfloat16).reshape(BATCH * SEQ, inner_width)
        group_part = jnp.dot(normed, w_out.T, preferred_element_type=jnp.float32).astype(jnp.bfloat16)
        group_part = lax.optimization_barrier(group_part)
        return (total + group_part.astype(jnp.float32), (projected, step_raw))
    total, (proj_all, raw_all) = lax.scan(add_group, jnp.zeros((BATCH * SEQ, D), jnp.float32), jnp.arange(N_TENSOR, dtype=jnp.int32))
    student = total.astype(jnp.bfloat16).reshape(BATCH, SEQ, D)
    gap = student.astype(jnp.float32) - teacher.astype(jnp.float32)
    sq_error = lax.optimization_barrier(jnp.mean(gap * gap, axis=-1))
    grad_student = (gap * (1.0 / math.sqrt(BATCH * SEQ))).astype(jnp.bfloat16)
    grad_flat = grad_student.reshape(BATCH * SEQ, D)

    def backward(inputs):
        group_index, projected, step_raw = inputs
        w_in, w_out, w_step, params, in_pick, out_pick = weights_of(group_index)
        d_normed = jnp.dot(grad_flat, w_out, preferred_element_type=jnp.float32).reshape(BATCH, SEQ, inner_width)

        def pull_one(values, raws, cotangent):
            normed_exact, pull_back = jax.vjp(lambda inner_values: state_mixer(inner_values, raws, *params), values.astype(jnp.float32))
            return (normed_exact, pull_back(cotangent)[0])
        normed_exact, d_projected = jax.vmap(pull_one)(projected, step_raw, d_normed)
        d_projected = d_projected.astype(jnp.bfloat16)
        normed = normed_exact.astype(jnp.bfloat16)
        in_terms = jnp.einsum('bsi,bsc->bic', tokens.astype(jnp.float32), d_projected.astype(jnp.float32)).astype(jnp.bfloat16)
        in_terms = lax.optimization_barrier(in_terms)
        in_sum = lax.optimization_barrier(jnp.sum(in_terms.astype(jnp.float32), axis=0))
        out_terms = jnp.einsum('bsd,bse->bde', grad_student.astype(jnp.float32), normed.astype(jnp.float32)).astype(jnp.bfloat16)
        out_terms = lax.optimization_barrier(out_terms)
        out_sum = lax.optimization_barrier(jnp.sum(out_terms.astype(jnp.float32), axis=0))
        return (keep_blocks(in_sum, in_pick), keep_blocks(out_sum, out_pick))
    in_parts, out_parts = lax.map(backward, (jnp.arange(N_TENSOR, dtype=jnp.int32), proj_all, raw_all))
    in_grad = jnp.transpose(in_parts, (1, 0, 2)).reshape(D, N_TENSOR * KEEP_IN * BLOCK)
    out_grad = jnp.transpose(out_parts, (1, 0, 2)).reshape(D, N_TENSOR * KEEP_OUT * BLOCK)
    return (sq_error, in_grad, out_grad)
```

```python
import functools
import math

import jax
import jax.numpy as jnp
from jax import lax
from jax.experimental import pallas as pl
from jax.experimental.pallas import tpu as pltpu
from jax.sharding import PartitionSpec as P

BLOCK = 128
VMEM = 48 * 1024 * 1024


def chunk_of(size, most):
    chunk = min(size, most)
    while size % chunk:
        chunk //= 2
    return chunk


def spread_into(dense_ref, blocks_ref, cols_ref, first, keep):
    dense_ref[...] = jnp.zeros_like(dense_ref)
    for i in range(dense_ref.shape[0] // BLOCK):
        rows = slice(i * BLOCK, (i + 1) * BLOCK)
        for k in range(keep):
            c = cols_ref[(first + i) * keep + k]
            dense_ref[rows, pl.ds(pl.multiple_of(c * BLOCK, BLOCK), BLOCK)] = blocks_ref[
                rows, k * BLOCK : (k + 1) * BLOCK
            ]


def contract_kernel(keep, cols_ref, x_ref, blocks_ref, out_ref, dense_ref, acc_ref):
    j = pl.program_id(0)
    spread_into(dense_ref, blocks_ref, cols_ref, j * (dense_ref.shape[0] // BLOCK), keep)
    term = jnp.dot(x_ref[...], dense_ref[...], preferred_element_type=jnp.float32)

    @pl.when(j == 0)
    def _():
        acc_ref[...] = term

    @pl.when(j > 0)
    def _():
        acc_ref[...] += term

    @pl.when(j == pl.num_programs(0) - 1)
    def _():
        out_ref[...] = acc_ref[...].astype(out_ref.dtype)


def contract(x, blocks, cols, out_dtype):
    seq, depth = x.shape
    keep = cols.shape[1]
    width = 2 * keep * BLOCK
    step = chunk_of(depth, 512)
    return pl.pallas_call(
        functools.partial(contract_kernel, keep),
        out_shape=jax.ShapeDtypeStruct((seq, width), out_dtype),
        grid_spec=pltpu.PrefetchScalarGridSpec(
            num_scalar_prefetch=1,
            grid=(depth // step,),
            in_specs=[
                pl.BlockSpec((seq, step), lambda j, c: (0, j)),
                pl.BlockSpec((step, keep * BLOCK), lambda j, c: (j, 0)),
            ],
            out_specs=pl.BlockSpec((seq, width), lambda j, c: (0, 0)),
            scratch_shapes=[
                pltpu.VMEM((step, width), jnp.bfloat16),
                pltpu.VMEM((seq, width), jnp.float32),
            ],
        ),
        compiler_params=pltpu.CompilerParams(vmem_limit_bytes=VMEM),
        cost_estimate=pl.CostEstimate(
            flops=2 * seq * depth * width,
            bytes_accessed=2 * depth * (seq + keep * BLOCK) + 4 * seq * width,
            transcendentals=0,
        ),
    )(cols.reshape(-1), x, blocks)


def expand_kernel(keep, cols_ref, x_ref, blocks_ref, out_ref, dense_ref):
    j = pl.program_id(0)
    spread_into(dense_ref, blocks_ref, cols_ref, j * (dense_ref.shape[0] // BLOCK), keep)
    out_ref[...] = lax.dot_general(
        x_ref[...], dense_ref[...], (((1,), (1,)), ((), ())), preferred_element_type=jnp.float32
    ).astype(out_ref.dtype)


def expand(x, blocks, cols):
    seq, width = x.shape
    rows = blocks.shape[0]
    keep = cols.shape[1]
    step = chunk_of(rows, 512)
    return pl.pallas_call(
        functools.partial(expand_kernel, keep),
        out_shape=jax.ShapeDtypeStruct((seq, rows), jnp.bfloat16),
        grid_spec=pltpu.PrefetchScalarGridSpec(
            num_scalar_prefetch=1,
            grid=(rows // step,),
            in_specs=[
                pl.BlockSpec((seq, width), lambda j, c: (0, 0)),
                pl.BlockSpec((step, keep * BLOCK), lambda j, c: (j, 0)),
            ],
            out_specs=pl.BlockSpec((seq, step), lambda j, c: (0, j)),
            scratch_shapes=[pltpu.VMEM((step, width), jnp.bfloat16)],
        ),
        compiler_params=pltpu.CompilerParams(vmem_limit_bytes=VMEM),
        cost_estimate=pl.CostEstimate(
            flops=2 * seq * rows * width,
            bytes_accessed=2 * rows * (seq + keep * BLOCK) + 2 * seq * width,
            transcendentals=0,
        ),
    )(cols.reshape(-1), x, blocks)


def kept_kernel(keep, pieces, base_ref, cols_ref, *refs):
    xs, ys = refs[:pieces], refs[pieces : 2 * pieces]
    out_ref, dense_ref = refs[2 * pieces :]
    j = pl.program_id(0)
    total = None
    for x_ref, y_ref in zip(xs, ys):
        term = lax.dot_general(
            x_ref[...], y_ref[...], (((0,), (0,)), ((), ())), preferred_element_type=jnp.float32
        )
        total = term if total is None else total + term
    dense_ref[...] = total
    block_rows = dense_ref.shape[0] // BLOCK
    for i in range(block_rows):
        rows = slice(i * BLOCK, (i + 1) * BLOCK)
        for k in range(keep):
            c = cols_ref[(j * block_rows + i) * keep + k]
            out_ref[rows, k * BLOCK : (k + 1) * BLOCK] = dense_ref[
                rows, pl.ds(pl.multiple_of(c * BLOCK, BLOCK), BLOCK)
            ]


def kept_product(wide, narrow, ys, position, cols):
    seq, rows = narrow[0].shape
    width = ys[0].shape[1]
    keep = cols.shape[1]
    step = chunk_of(rows, 256)
    steps = rows // step
    pieces = len(ys)
    xs = tuple(wide) + tuple(narrow)
    return pl.pallas_call(
        functools.partial(kept_kernel, keep, pieces),
        out_shape=jax.ShapeDtypeStruct((rows, keep * BLOCK), jnp.float32),
        grid_spec=pltpu.PrefetchScalarGridSpec(
            num_scalar_prefetch=2,
            grid=(steps,),
            in_specs=[pl.BlockSpec((seq, step), lambda j, b, c: (0, b[0] * steps + j))] * len(wide)
            + [pl.BlockSpec((seq, step), lambda j, b, c: (0, j))] * len(narrow)
            + [pl.BlockSpec((seq, width), lambda j, b, c: (0, 0))] * pieces,
            out_specs=pl.BlockSpec((step, keep * BLOCK), lambda j, b, c: (j, 0)),
            scratch_shapes=[pltpu.VMEM((step, width), jnp.float32)],
        ),
        compiler_params=pltpu.CompilerParams(vmem_limit_bytes=VMEM),
        cost_estimate=pl.CostEstimate(
            flops=2 * seq * pieces * rows * width,
            bytes_accessed=2 * seq * pieces * (rows + width) + 4 * rows * keep * BLOCK,
            transcendentals=0,
        ),
    )(position.reshape(1), cols.reshape(-1), *xs, *ys)


def state_mixer(projected, step_raw, conv_taps, step_bias, decay_rate, skip_gain, norm_gain):
    seq_steps = projected.shape[0]
    chan_count = projected.shape[1]
    inner_width = norm_gain.shape[0]
    head_count = step_bias.shape[0]
    head_width = inner_width // head_count
    state_size = (chan_count - inner_width) // 2
    taps = conv_taps.shape[0]
    padded = jnp.concatenate([jnp.zeros((taps - 1, chan_count), jnp.float32), projected], 0)
    conv_sum = jnp.zeros((seq_steps, chan_count), jnp.float32)
    for offset in range(taps):
        conv_sum = conv_sum + conv_taps[offset][None, :] * padded[offset : offset + seq_steps]
    activated = jax.nn.silu(conv_sum)
    head_inputs = activated[:, :inner_width].reshape(seq_steps, head_count, head_width)
    state_in = activated[:, inner_width : inner_width + state_size]
    state_out = activated[:, inner_width + state_size :]
    step_size = jax.nn.softplus(step_raw + step_bias[None, :])
    log_decay = jnp.cumsum(-decay_rate[None, :] * step_size, axis=0)
    scores = jnp.dot(state_out, state_in.T, precision=lax.Precision.HIGHEST)
    later = (jnp.arange(seq_steps)[:, None] >= jnp.arange(seq_steps)[None, :])[:, :, None]
    log_gap = log_decay[:, None, :] - log_decay[None, :, :]
    decay = jnp.where(later, jnp.exp(jnp.where(later, log_gap, 0.0)), 0.0)
    weights = scores[:, :, None] * decay * step_size[None, :, :]
    mixed = jnp.einsum("tsh,shp->thp", weights, head_inputs, precision=lax.Precision.HIGHEST)
    mixed = mixed + skip_gain[None, :, None] * head_inputs
    flat = mixed.reshape(seq_steps, inner_width)
    scale = lax.rsqrt(jnp.mean(flat * flat, axis=1, keepdims=True) + 1e-05)
    return flat * scale * norm_gain[None, :]


def shifted(value, axis, shift):
    size = lax.axis_size(axis)
    return lax.ppermute(value, axis, [(i, (i + shift) % size) for i in range(size)])


def after(value, *earlier):
    return lax.optimization_barrier((value,) + earlier)[0]


def local(
    tokens,
    teacher,
    in_blocks,
    in_columns,
    step_weight,
    out_blocks,
    out_columns,
    conv_weight,
    step_bias,
    decay_rate,
    skip_gain,
    norm_gain,
):
    my_tokens = tokens[0]
    my_teacher = teacher[0]
    seq_len, model_width = my_tokens.shape
    ring = lax.axis_size("fsdp")
    cores = lax.axis_size("dp")
    me = lax.axis_index("fsdp")
    core = lax.axis_index("dp")
    width = model_width // ring
    part = width // cores
    block_rows = part // BLOCK
    shifts = range(1, ring)

    def columns_for(value, shift):
        return lax.dynamic_slice_in_dim(value, lax.rem(me + shift, ring) * width, width, 1)

    def to_cores(values):
        sent = []
        for shift in range(1, cores):
            start = lax.rem(core + shift, cores) * part
            for value in values:
                piece = lax.dynamic_slice_in_dim(value, start, part, 1)
                sent.append(shifted(piece, "dp", shift))
        return sent

    def all_cores(values):
        return [shifted(value, "dp", shift) for shift in range(1, cores) for value in values]

    token_parts = [columns_for(my_tokens, 0)]
    token_parts += [shifted(columns_for(my_tokens, s), "fsdp", s) for s in shifts]

    in_own = contract(token_parts[0], in_blocks, in_columns, jnp.float32)
    raw_own = jnp.dot(token_parts[0], step_weight, preferred_element_type=jnp.float32)
    projected_sum, step_raw = in_own, raw_own
    for s in shifts:
        partial = contract(token_parts[s], in_blocks, in_columns, jnp.bfloat16)
        raw = jnp.dot(token_parts[s], step_weight, preferred_element_type=jnp.float32)
        projected_sum = projected_sum + shifted(partial, "fsdp", -s).astype(jnp.float32)
        step_raw = step_raw + shifted(raw, "fsdp", -s)
    projected = projected_sum.astype(jnp.bfloat16)

    def local_mix(values):
        return state_mixer(
            values, step_raw, conv_weight, step_bias, decay_rate, skip_gain, norm_gain
        )

    normed_exact, pull_back = jax.vjp(local_mix, projected.astype(jnp.float32))
    normed = normed_exact.astype(jnp.bfloat16)
    normed_parts = [normed] + [shifted(normed, "fsdp", s) for s in shifts]

    teacher_parts = [columns_for(my_teacher, 0)]
    teacher_parts += [
        shifted(after(columns_for(my_teacher, s), normed_parts[s]), "fsdp", s) for s in shifts
    ]
    token_rest = to_cores([after(value, normed) for value in token_parts])
    normed_rest = all_cores(normed_parts)

    total_tokens = seq_len * ring * cores
    grads, errors, backs = [], [], []
    students = []
    for value in normed_parts:
        term = expand(value, out_blocks, out_columns)
        if students:
            term = after(term, students[-1])
        students.append(lax.psum(term, "tensor"))
    for s in range(ring):
        gap = students[s].astype(jnp.float32) - teacher_parts[s].astype(jnp.float32)
        errors.append(jnp.sum(gap * gap, axis=1)[None, :])
        grads.append((gap * (1.0 / math.sqrt(total_tokens))).astype(jnp.bfloat16))
        backs.append(
            contract(
                grads[s], out_blocks, out_columns, jnp.float32 if s == 0 else jnp.bfloat16
            )
        )
    sq_error, d_normed = errors[0], backs[0]
    for s in shifts:
        d_normed = d_normed + shifted(backs[s], "fsdp", -s).astype(jnp.float32)
        sq_error = sq_error + shifted(errors[s], "fsdp", -s)
    sq_error = sq_error * (1.0 / model_width)

    in_pick = lax.dynamic_slice_in_dim(in_columns, core * block_rows, block_rows, 0)
    out_pick = lax.dynamic_slice_in_dim(out_columns, core * block_rows, block_rows, 0)
    grad_rest = to_cores(grads)
    out_grad = kept_product(grads, grad_rest, normed_parts + normed_rest, core, out_pick)

    d_projected = pull_back(d_normed)[0].astype(jnp.bfloat16)
    d_parts = [d_projected] + [shifted(d_projected, "fsdp", s) for s in shifts]
    d_rest = all_cores(d_parts)
    in_grad = kept_product(token_parts, token_rest, d_parts + d_rest, core, in_pick)
    return (sq_error, in_grad, out_grad)


def solution(mesh):
    placed = (
        P(("groups", "fsdp", "dp"), None, None),
        P(("groups", "fsdp", "dp"), None, None),
        P("fsdp", "tensor"),
        P("fsdp", "tensor"),
        P("fsdp", "tensor"),
        P("fsdp", "tensor"),
        P("fsdp", "tensor"),
        P(None, "tensor"),
        P("tensor"),
        P("tensor"),
        P("tensor"),
        P("tensor"),
    )
    return jax.shard_map(
        local,
        mesh=mesh,
        in_specs=placed,
        out_specs=(
            P(("groups", "fsdp", "dp"), None),
            P(("groups", "fsdp", "dp"), "tensor"),
            P(("groups", "fsdp", "dp"), "tensor"),
        ),
        check_vma=False,
    )
```

```python
import functools
import math

import jax
import jax.numpy as jnp
from jax import lax
from jax.experimental import pallas as pl
from jax.experimental.pallas import tpu as pltpu
from jax.sharding import PartitionSpec as P

BLOCK = 128
VMEM = 48 * 1024 * 1024


def chunk_of(size, most):
    chunk = min(size, most)
    while size % chunk:
        chunk //= 2
    return chunk


def spread_into(dense_ref, blocks_ref, cols_ref, first, keep):
    dense_ref[...] = jnp.zeros_like(dense_ref)
    for i in range(dense_ref.shape[0] // BLOCK):
        rows = slice(i * BLOCK, (i + 1) * BLOCK)
        for k in range(keep):
            c = cols_ref[(first + i) * keep + k]
            dense_ref[rows, pl.ds(pl.multiple_of(c * BLOCK, BLOCK), BLOCK)] = blocks_ref[
                rows, k * BLOCK : (k + 1) * BLOCK
            ]


def contract_kernel(keep, cols_ref, x_ref, blocks_ref, out_ref, dense_ref, acc_ref):
    j = pl.program_id(0)
    spread_into(dense_ref, blocks_ref, cols_ref, j * (dense_ref.shape[0] // BLOCK), keep)
    term = jnp.dot(x_ref[...], dense_ref[...], preferred_element_type=jnp.float32)

    @pl.when(j == 0)
    def _():
        acc_ref[...] = term

    @pl.when(j > 0)
    def _():
        acc_ref[...] += term

    @pl.when(j == pl.num_programs(0) - 1)
    def _():
        out_ref[...] = acc_ref[...].astype(out_ref.dtype)


def contract(x, blocks, cols, out_dtype):
    seq, depth = x.shape
    keep = cols.shape[1]
    width = 2 * keep * BLOCK
    step = chunk_of(depth, 512)
    return pl.pallas_call(
        functools.partial(contract_kernel, keep),
        out_shape=jax.ShapeDtypeStruct((seq, width), out_dtype),
        grid_spec=pltpu.PrefetchScalarGridSpec(
            num_scalar_prefetch=1,
            grid=(depth // step,),
            in_specs=[
                pl.BlockSpec((seq, step), lambda j, c: (0, j)),
                pl.BlockSpec((step, keep * BLOCK), lambda j, c: (j, 0)),
            ],
            out_specs=pl.BlockSpec((seq, width), lambda j, c: (0, 0)),
            scratch_shapes=[
                pltpu.VMEM((step, width), jnp.bfloat16),
                pltpu.VMEM((seq, width), jnp.float32),
            ],
        ),
        compiler_params=pltpu.CompilerParams(vmem_limit_bytes=VMEM),
        cost_estimate=pl.CostEstimate(
            flops=2 * seq * depth * width,
            bytes_accessed=2 * depth * (seq + keep * BLOCK) + 4 * seq * width,
            transcendentals=0,
        ),
    )(cols.reshape(-1), x, blocks)


def expand_kernel(keep, cols_ref, x_ref, blocks_ref, out_ref, dense_ref):
    j = pl.program_id(0)
    spread_into(dense_ref, blocks_ref, cols_ref, j * (dense_ref.shape[0] // BLOCK), keep)
    out_ref[...] = lax.dot_general(
        x_ref[...], dense_ref[...], (((1,), (1,)), ((), ())), preferred_element_type=jnp.float32
    ).astype(out_ref.dtype)


def expand(x, blocks, cols):
    seq, width = x.shape
    rows = blocks.shape[0]
    keep = cols.shape[1]
    step = chunk_of(rows, 512)
    return pl.pallas_call(
        functools.partial(expand_kernel, keep),
        out_shape=jax.ShapeDtypeStruct((seq, rows), jnp.bfloat16),
        grid_spec=pltpu.PrefetchScalarGridSpec(
            num_scalar_prefetch=1,
            grid=(rows // step,),
            in_specs=[
                pl.BlockSpec((seq, width), lambda j, c: (0, 0)),
                pl.BlockSpec((step, keep * BLOCK), lambda j, c: (j, 0)),
            ],
            out_specs=pl.BlockSpec((seq, step), lambda j, c: (0, j)),
            scratch_shapes=[pltpu.VMEM((step, width), jnp.bfloat16)],
        ),
        compiler_params=pltpu.CompilerParams(vmem_limit_bytes=VMEM),
        cost_estimate=pl.CostEstimate(
            flops=2 * seq * rows * width,
            bytes_accessed=2 * rows * (seq + keep * BLOCK) + 2 * seq * width,
            transcendentals=0,
        ),
    )(cols.reshape(-1), x, blocks)


def kept_kernel(keep, pieces, base_ref, cols_ref, *refs):
    xs, ys = refs[:pieces], refs[pieces : 2 * pieces]
    out_ref, dense_ref = refs[2 * pieces :]
    j = pl.program_id(0)
    total = None
    for x_ref, y_ref in zip(xs, ys):
        term = lax.dot_general(
            x_ref[...], y_ref[...], (((0,), (0,)), ((), ())), preferred_element_type=jnp.float32
        )
        total = term if total is None else total + term
    dense_ref[...] = total
    block_rows = dense_ref.shape[0] // BLOCK
    for i in range(block_rows):
        rows = slice(i * BLOCK, (i + 1) * BLOCK)
        for k in range(keep):
            c = cols_ref[(j * block_rows + i) * keep + k]
            out_ref[rows, k * BLOCK : (k + 1) * BLOCK] = dense_ref[
                rows, pl.ds(pl.multiple_of(c * BLOCK, BLOCK), BLOCK)
            ]


def kept_product(wide, narrow, ys, position, cols):
    seq, rows = narrow[0].shape
    width = ys[0].shape[1]
    keep = cols.shape[1]
    step = chunk_of(rows, 256)
    steps = rows // step
    pieces = len(ys)
    xs = tuple(wide) + tuple(narrow)
    return pl.pallas_call(
        functools.partial(kept_kernel, keep, pieces),
        out_shape=jax.ShapeDtypeStruct((rows, keep * BLOCK), jnp.float32),
        grid_spec=pltpu.PrefetchScalarGridSpec(
            num_scalar_prefetch=2,
            grid=(steps,),
            in_specs=[pl.BlockSpec((seq, step), lambda j, b, c: (0, b[0] * steps + j))] * len(wide)
            + [pl.BlockSpec((seq, step), lambda j, b, c: (0, j))] * len(narrow)
            + [pl.BlockSpec((seq, width), lambda j, b, c: (0, 0))] * pieces,
            out_specs=pl.BlockSpec((step, keep * BLOCK), lambda j, b, c: (j, 0)),
            scratch_shapes=[pltpu.VMEM((step, width), jnp.float32)],
        ),
        compiler_params=pltpu.CompilerParams(vmem_limit_bytes=VMEM),
        cost_estimate=pl.CostEstimate(
            flops=2 * seq * pieces * rows * width,
            bytes_accessed=2 * seq * pieces * (rows + width) + 4 * rows * keep * BLOCK,
            transcendentals=0,
        ),
    )(position.reshape(1), cols.reshape(-1), *xs, *ys)


def state_mixer(projected, step_raw, conv_taps, step_bias, decay_rate, skip_gain, norm_gain):
    seq_steps = projected.shape[0]
    chan_count = projected.shape[1]
    inner_width = norm_gain.shape[0]
    head_count = step_bias.shape[0]
    head_width = inner_width // head_count
    state_size = (chan_count - inner_width) // 2
    taps = conv_taps.shape[0]
    padded = jnp.concatenate([jnp.zeros((taps - 1, chan_count), jnp.float32), projected], 0)
    conv_sum = jnp.zeros((seq_steps, chan_count), jnp.float32)
    for offset in range(taps):
        conv_sum = conv_sum + conv_taps[offset][None, :] * padded[offset : offset + seq_steps]
    activated = jax.nn.silu(conv_sum)
    head_inputs = activated[:, :inner_width].reshape(seq_steps, head_count, head_width)
    state_in = activated[:, inner_width : inner_width + state_size]
    state_out = activated[:, inner_width + state_size :]
    step_size = jax.nn.softplus(step_raw + step_bias[None, :])
    log_decay = jnp.cumsum(-decay_rate[None, :] * step_size, axis=0)
    scores = jnp.dot(state_out, state_in.T, precision=lax.Precision.HIGHEST)
    later = (jnp.arange(seq_steps)[:, None] >= jnp.arange(seq_steps)[None, :])[:, :, None]
    log_gap = log_decay[:, None, :] - log_decay[None, :, :]
    decay = jnp.where(later, jnp.exp(jnp.where(later, log_gap, 0.0)), 0.0)
    weights = scores[:, :, None] * decay * step_size[None, :, :]
    mixed = jnp.einsum("tsh,shp->thp", weights, head_inputs, precision=lax.Precision.HIGHEST)
    mixed = mixed + skip_gain[None, :, None] * head_inputs
    flat = mixed.reshape(seq_steps, inner_width)
    scale = lax.rsqrt(jnp.mean(flat * flat, axis=1, keepdims=True) + 1e-05)
    return flat * scale * norm_gain[None, :]


def shifted(value, axis, shift):
    size = lax.axis_size(axis)
    return lax.ppermute(value, axis, [(i, (i + shift) % size) for i in range(size)])


def after(value, *earlier):
    return lax.optimization_barrier((value,) + earlier)[0]


def line_sum(value, axis):
    size = lax.axis_size(axis)
    me = lax.axis_index(axis)
    rows = value.shape[0] // size

    def chunk(index):
        index = jnp.clip(index, 0, size - 1)
        return lax.dynamic_slice_in_dim(value, index * rows, rows, 0)

    def add(left, right):
        return (left.astype(jnp.float32) + right.astype(jnp.float32)).astype(value.dtype)

    up = down = None
    for s in range(1, size):
        to_up, to_down = chunk(me + size - s), chunk(me - size + s)
        if up is not None:
            to_up, to_down = add(to_up, up), add(to_down, down)
        pairs = [(i, i + 1) for i in range(min(s, size - 1))]
        up = lax.ppermute(to_up, axis, pairs)
        down = lax.ppermute(to_down, axis, [(size - 1 - i, size - 1 - j) for i, j in pairs])
    mine = chunk(me).astype(jnp.float32)
    if up is not None:
        mine = mine + up.astype(jnp.float32) + down.astype(jnp.float32)
    mine = mine.astype(value.dtype)

    from_below, from_above = {}, {}
    up = down = mine
    for s in range(1, size):
        pairs = [(i, i + 1) for i in range(s - 1, size - 1)]
        up = lax.ppermute(up, axis, pairs)
        down = lax.ppermute(down, axis, [(size - 1 - i, size - 1 - j) for i, j in pairs])
        from_below[s], from_above[s] = up, down
    total = lax.dynamic_update_slice_in_dim(jnp.zeros_like(value), mine, me * rows, 0)
    for s in range(1, size):
        piece = jnp.where(me >= s, from_below[s], from_above[size - s])
        total = lax.dynamic_update_slice_in_dim(
            total, piece, lax.rem(me - s + size, size) * rows, 0
        )
    return total


def local(
    tokens,
    teacher,
    in_blocks,
    in_columns,
    step_weight,
    out_blocks,
    out_columns,
    conv_weight,
    step_bias,
    decay_rate,
    skip_gain,
    norm_gain,
):
    my_tokens = tokens[0]
    my_teacher = teacher[0]
    seq_len, model_width = my_tokens.shape
    ring = lax.axis_size("fsdp")
    cores = lax.axis_size("dp")
    me = lax.axis_index("fsdp")
    core = lax.axis_index("dp")
    width = model_width // ring
    part = width // cores
    block_rows = part // BLOCK
    shifts = range(1, ring)

    def columns_for(value, shift):
        return lax.dynamic_slice_in_dim(value, lax.rem(me + shift, ring) * width, width, 1)

    def to_cores(values):
        sent = []
        for shift in range(1, cores):
            start = lax.rem(core + shift, cores) * part
            for value in values:
                piece = lax.dynamic_slice_in_dim(value, start, part, 1)
                sent.append(shifted(piece, "dp", shift))
        return sent

    def all_cores(values):
        return [shifted(value, "dp", shift) for shift in range(1, cores) for value in values]

    token_parts = [columns_for(my_tokens, 0)]
    token_parts += [shifted(columns_for(my_tokens, s), "fsdp", s) for s in shifts]

    in_own = contract(token_parts[0], in_blocks, in_columns, jnp.float32)
    raw_own = jnp.dot(token_parts[0], step_weight, preferred_element_type=jnp.float32)
    projected_sum, step_raw = in_own, raw_own
    for s in shifts:
        partial = contract(token_parts[s], in_blocks, in_columns, jnp.bfloat16)
        raw = jnp.dot(token_parts[s], step_weight, preferred_element_type=jnp.float32)
        projected_sum = projected_sum + shifted(partial, "fsdp", -s).astype(jnp.float32)
        step_raw = step_raw + shifted(raw, "fsdp", -s)
    projected = projected_sum.astype(jnp.bfloat16)

    def local_mix(values):
        return state_mixer(
            values, step_raw, conv_weight, step_bias, decay_rate, skip_gain, norm_gain
        )

    normed_exact, pull_back = jax.vjp(local_mix, projected.astype(jnp.float32))
    normed = normed_exact.astype(jnp.bfloat16)
    normed_parts = [normed] + [shifted(normed, "fsdp", s) for s in shifts]

    teacher_parts = [columns_for(my_teacher, 0)]
    teacher_parts += [
        shifted(after(columns_for(my_teacher, s), normed_parts[s]), "fsdp", s) for s in shifts
    ]
    token_rest = to_cores([after(value, normed) for value in token_parts])
    normed_rest = all_cores(normed_parts)

    total_tokens = seq_len * ring * cores
    grads, errors, backs = [], [], []
    students = [
        line_sum(expand(value, out_blocks, out_columns), "tensor") for value in normed_parts
    ]
    for s in range(ring):
        gap = students[s].astype(jnp.float32) - teacher_parts[s].astype(jnp.float32)
        errors.append(jnp.sum(gap * gap, axis=1)[None, :])
        grads.append((gap * (1.0 / math.sqrt(total_tokens))).astype(jnp.bfloat16))
        backs.append(
            contract(
                grads[s], out_blocks, out_columns, jnp.float32 if s == 0 else jnp.bfloat16
            )
        )
    sq_error, d_normed = errors[0], backs[0]
    for s in shifts:
        d_normed = d_normed + shifted(backs[s], "fsdp", -s).astype(jnp.float32)
        sq_error = sq_error + shifted(errors[s], "fsdp", -s)
    sq_error = sq_error * (1.0 / model_width)

    in_pick = lax.dynamic_slice_in_dim(in_columns, core * block_rows, block_rows, 0)
    out_pick = lax.dynamic_slice_in_dim(out_columns, core * block_rows, block_rows, 0)
    grad_rest = to_cores(grads)
    out_grad = kept_product(grads, grad_rest, normed_parts + normed_rest, core, out_pick)

    d_normed = after(d_normed, *grad_rest, *token_rest, *normed_rest)
    d_projected = pull_back(d_normed)[0].astype(jnp.bfloat16)
    d_parts = [d_projected]
    d_parts += [after(shifted(d_projected, "fsdp", s), out_grad) for s in shifts]
    d_rest = all_cores(d_parts)
    in_grad = kept_product(token_parts, token_rest, d_parts + d_rest, core, in_pick)
    return (sq_error, in_grad, out_grad)


def solution(mesh):
    placed = (
        P(("groups", "fsdp", "dp"), None, None),
        P(("groups", "fsdp", "dp"), None, None),
        P("fsdp", "tensor"),
        P("fsdp", "tensor"),
        P("fsdp", "tensor"),
        P("fsdp", "tensor"),
        P("fsdp", "tensor"),
        P(None, "tensor"),
        P("tensor"),
        P("tensor"),
        P("tensor"),
        P("tensor"),
    )
    return jax.shard_map(
        local,
        mesh=mesh,
        in_specs=placed,
        out_specs=(
            P(("groups", "fsdp", "dp"), None),
            P(("groups", "fsdp", "dp"), "tensor"),
            P(("groups", "fsdp", "dp"), "tensor"),
        ),
        check_vma=False,
    )
```
